256 devices in a mesh: tm: 32 (over z, y), row: 8 (over x, core).
Axes of the slice: x: 4, y: 4, z: 8, core: 2. Of those that a mesh axis runs over, the one named last changes fastest.
Arguments:
- tokens: bfloat16 [32768, 3072], P(('tm', 'row')), may hold values from -6 to 6
- w_qkv: bfloat16 [3072, 3, 3072], P(None, None, 'row'), may hold values from -1 to 1
- qk_gain: float32 [2, 3072], P(None, 'row'), may hold values from 0.5 to 6
- w_out: bfloat16 [3072, 3072], P('row'), may hold values from -0.109375 to 0.109375
- band_start: int32 [64, 5], replicated, may hold values from 0 to 2
Outputs:
- mixed: bfloat16 [32768, 3072], P(('tm', 'row'))
The draws below stay inside these ranges and needn't reach their ends.
All inputs are finite; a program needn't handle non-finite values.
Results may differ from the reference program's by a relative error of at most 0.019.
Values may be sent and summed in bfloat16 or wider, within the bound.
A program may use at most 128 MiB of HBM per device.

```python
import math
import jax
import jax.numpy as jnp
from jax import lax

D = 3072
HEADS = 24
HD = 128
S = 512
SB = 128
WSLOT = 2
FR_DEV = 2
NFAR = 5
F_ALL = 64
TOKENS = 32768
HEADS_DEV = 3
N_ROW = 8


def draw_tokens(key, part):
    key = jax.random.fold_in(key, 11)
    drawn = jax.random.normal(key, (TOKENS, D), jnp.float32)
    return jnp.clip(drawn, -6.0, 6.0).astype(jnp.bfloat16)


def draw_w_qkv(key, part):
    key = jax.random.fold_in(key, 12)
    query_key, key_key, value_key = jax.random.split(key, 3)
    factor = 1.0 / jnp.sqrt(jnp.float32(D))
    query_part = jax.random.normal(query_key, (D, D), jnp.float32) * factor
    key_part = jax.random.normal(key_key, (D, D), jnp.float32) * factor
    value_part = jax.random.normal(value_key, (D, D), jnp.float32) * factor
    stacked = jnp.stack([query_part, key_part, value_part], axis=1)
    return jnp.clip(stacked, -1.0, 1.0).astype(jnp.bfloat16)


def draw_qk_gain(key, part):
    key = jax.random.fold_in(key, 13)
    jitter_key = jax.random.fold_in(key, 1)
    gains = 1.0 + 0.2 * jax.random.uniform(jitter_key, (2, D), jnp.float32, -1.0, 1.0)
    return jnp.clip(gains, 0.5, 6.0)


def touch_ends(values, key, smallest, top_value):
    place = [jax.random.randint(jax.random.fold_in(key, axis), (), 0, length) for axis, length in enumerate(values.shape)]
    widest = values.shape.index(max(values.shape))
    next_to = place[:widest] + [(place[widest] + 1) % values.shape[widest]] + place[widest + 1:]
    return values.at[tuple(place)].set(smallest).at[tuple(next_to)].set(top_value)


def shard_levels(own_key, extent, cuts, smallest, high):
    level = 1.0
    for axis_at, shards_of in cuts:
        steps = jax.random.uniform(jax.random.fold_in(jax.random.fold_in(own_key, 6), axis_at), (shards_of,), jnp.float32, smallest / len(cuts), high / len(cuts))
        level = level * jnp.repeat(jnp.exp(steps), extent[axis_at] // shards_of).reshape((-1,) + (1,) * (len(extent) - 1 - axis_at))
    return level


def scatter_about(stream_key, shape, scale, bound, cuts=(), held_as=jnp.bfloat16):
    entries = scale * jax.random.normal(stream_key, shape, jnp.float32)
    if cuts:
        entries = entries * shard_levels(stream_key, shape, cuts, -0.22, 0.18)
    return jnp.clip(entries, -bound, bound).astype(held_as)


def setup_inputs(seed: int = 0) -> dict:
    key_list = jax.random.split(jax.random.key(seed), 6)
    return {
        "tokens": draw_tokens(jax.random.fold_in(key_list[5], 71), 0),
        "w_qkv": draw_w_qkv(jax.random.fold_in(key_list[5], 71), 0),
        "qk_gain": draw_qk_gain(jax.random.fold_in(key_list[5], 71), 0),
        "w_out": scatter_about(key_list[3], (D, D), D ** -0.5, 0.109375, ((0, 8),)),
        "band_start": touch_ends(jax.random.randint(key_list[4], (F_ALL, NFAR), 0, S // SB - WSLOT + 1), jax.random.fold_in(key_list[4], 1), 0, (S // SB - WSLOT + 1) - 1).astype(jnp.int32),
    }


def normalize(columns, gain_row, head_count):
    shaped = columns.reshape(columns.shape[0], head_count, HD)
    factor = lax.rsqrt(lax.optimization_barrier(jnp.mean(shaped * shaped, axis=-1, keepdims=True)) + 1e-06)
    scaled = shaped * factor * gain_row.reshape(head_count, HD)
    return scaled.reshape(columns.shape[0], head_count * HD).astype(jnp.bfloat16)

def attend(query_rows, key_rows, value_rows, usable, head_count):
    query_heads = query_rows.reshape(query_rows.shape[0], head_count, HD).astype(jnp.float32)
    key_heads = key_rows.reshape(key_rows.shape[0], head_count, HD).astype(jnp.float32)
    value_heads = value_rows.reshape(value_rows.shape[0], head_count, HD).astype(jnp.float32)
    scores = jnp.einsum('shd,khd->hsk', query_heads, key_heads) / math.sqrt(HD)
    scores = jnp.where(usable[None, None, :], scores, -1e+30)
    row_max = lax.optimization_barrier(jnp.max(scores, axis=-1, keepdims=True))
    weights = jnp.where(usable[None, None, :], jnp.exp(scores - row_max), 0.0)
    totals = lax.optimization_barrier(jnp.sum(weights, axis=-1))
    probabilities = weights.astype(jnp.bfloat16)
    mixed = jnp.einsum('hsk,khd->shd', probabilities.astype(jnp.float32), value_heads)
    mixed = mixed / jnp.transpose(totals)[:, :, None]
    return mixed.reshape(query_rows.shape[0], head_count * HD).astype(jnp.bfloat16)

def reference(tokens, w_qkv, qk_gain, w_out, band_start):
    joined = w_qkv.reshape(D, 3 * D)
    by_frame = tokens.reshape(F_ALL, S, D)

    def project(frame_tokens):
        merged = jnp.dot(frame_tokens, joined, preferred_element_type=jnp.float32)
        return (normalize(merged[:, :D], qk_gain[0], HEADS), normalize(merged[:, D:2 * D], qk_gain[1], HEADS), merged[:, 2 * D:].astype(jnp.bfloat16))
    queries, keys, values = lax.map(project, by_frame)
    flat_keys = keys.reshape(F_ALL * S, D)
    flat_values = values.reshape(F_ALL * S, D)

    def one_frame(query_frame):
        near_index = query_frame - 1 + jnp.arange(3, dtype=jnp.int32)
        near_valid = (near_index >= 0) & (near_index < F_ALL)
        safe_index = jnp.clip(near_index, 0, F_ALL - 1).astype(jnp.int32)
        key_parts = [keys[safe_index].reshape(3 * S, D)]
        value_parts = [values[safe_index].reshape(3 * S, D)]
        usable_parts = [jnp.repeat(near_valid, S)]
        for level in range(NFAR):
            rows_level = max(1, WSLOT // 2 ** level) * SB
            sign = jnp.where((query_frame + level) % 2 == 0, 1, -1).astype(jnp.int32)
            key_frame = (query_frame + sign * FR_DEV * 2 ** level).astype(jnp.int32)
            inside = (key_frame >= 0) & (key_frame < F_ALL)
            safe_frame = jnp.clip(key_frame, 0, F_ALL - 1).astype(jnp.int32)
            first = safe_frame * S + band_start[query_frame, level] * SB
            take_rows = (first + jnp.arange(rows_level, dtype=jnp.int32)).astype(jnp.int32)
            key_parts.append(flat_keys[take_rows])
            value_parts.append(flat_values[take_rows])
            usable_parts.append(jnp.broadcast_to(inside, (rows_level,)))
        usable = jnp.concatenate(usable_parts)
        key_rows = jnp.concatenate(key_parts, axis=0)
        value_rows = jnp.concatenate(value_parts, axis=0)
        return attend(queries[query_frame], key_rows, value_rows, usable, HEADS)
    attended = lax.map(one_frame, jnp.arange(F_ALL, dtype=jnp.int32)).reshape(TOKENS, D)
    group_width = HEADS_DEV * HD
    summed = jnp.zeros((TOKENS, D), jnp.float32)
    for group_index in range(N_ROW):
        lower = group_index * group_width
        partial_value = jnp.dot(attended[:, lower:lower + group_width], w_out[lower:lower + group_width], preferred_element_type=jnp.float32).astype(jnp.bfloat16)
        partial_value = lax.optimization_barrier(partial_value)
        summed = summed + partial_value.astype(jnp.float32)
    return summed.astype(jnp.bfloat16)
```

```python
import functools
import math

import jax
import jax.numpy as jnp
from jax import lax
from jax.experimental import pallas as pl
from jax.experimental.pallas import tpu as pltpu
from jax.sharding import PartitionSpec as P

MESH = pl.DeviceIdType.MESH
D = 3072
HD = 128
HL = 3
W = HL * HD
TB = 128
CH = 2 * TB
ROWS = 4 * CH
N_TM = 32
LO, OWN, HI, FAR, FAR4, BAND0 = 0, 512, 1536, 2048, 2816, 2944
KV_ROWS = 3456
QSCALE = math.log2(math.e) / math.sqrt(HD)
NEG = -1e30
KB = 256
F32 = jnp.float32
BF16 = jnp.bfloat16


def mo(value, by):
    return pl.multiple_of(value, by)


def kernel(
    tok, w3, gain, wout, band, out,
    G, WQ, WO, Q, KV, FS, ACC, MX, LS, S, PB, AF, A2, P0, P1, P2, P3, RU, RD, RL, RR,
    loc, sx, rx, sd, rd, sn, rn, sf, rf, sa, ra, sr, rr,
):
    tm = lax.axis_index("tm")
    row = lax.axis_index("row")
    x = row // 2
    c = row % 2
    right = (x + 1) % 4
    left = (x + 3) % 4
    across = (x + 2) % 4
    d_right = (tm, right * 2 + c)
    d_left = (tm, left * 2 + c)
    d_core = (tm, x * 2 + (1 - c))

    def d_tm(shift):
        return ((tm + shift + N_TM) % N_TM, row)

    loads = [pltpu.make_async_copy(tok, G.at[pl.ds(mo(row * TB, TB), TB)], loc.at[0])]
    for j in range(3):
        loads.append(pltpu.make_async_copy(w3.at[j], WQ.at[:, pl.ds(j * W, W)], loc.at[1 + j]))
    loads.append(pltpu.make_async_copy(wout, WO.at[pl.ds(0, W)], loc.at[4]))
    for load in loads:
        load.start()

    partners = [d_right, d_left, d_core, d_tm(1), d_tm(-1), d_tm(2), d_tm(-2),
                d_tm(4), d_tm(-4), d_tm(8), d_tm(-8), d_tm(16)]
    barrier = pltpu.get_barrier_semaphore()
    for device in partners:
        pl.semaphore_signal(barrier, inc=1, device_id=device, device_id_type=MESH)
    pl.semaphore_wait(barrier, len(partners))

    def remote(src, dst, send, recv, device):
        return pltpu.make_async_remote_copy(
            src_ref=src, dst_ref=dst, send_sem=send, recv_sem=recv,
            device_id=device, device_id_type=MESH)

    sent = []

    def send(src, dst, send_sem, recv_sem, device):
        copy = remote(src, dst, send_sem, recv_sem, device)
        copy.start()
        sent.append(copy)

    def arrived(dst, recv_sem, send_sem):
        remote(dst, dst, send_sem, recv_sem, d_core).wait_recv()

    H = TB // 2

    def half(xx, cc, part):
        return G.at[pl.ds(mo(((xx * 2 + cc) * 2 + part) * H, H), H)]

    send(tok.at[pl.ds(0, H)], half(x, c, 0), sx.at[0], rx.at[0], d_right)
    send(tok.at[pl.ds(H, H)], half(x, c, 1), sx.at[2], rx.at[2], d_left)
    send(tok, G.at[pl.ds(mo(row * TB, TB), TB)], sd.at[6], rd.at[6], d_core)
    send(tok.at[pl.ds(H, H)], half(x, c, 1), sx.at[1], rx.at[1], d_right)
    send(tok.at[pl.ds(0, H)], half(x, c, 0), sx.at[3], rx.at[3], d_left)
    send(wout, WO.at[pl.ds(W, W)], sd.at[7], rd.at[7], d_core)

    def pass_on(k, xx, part, device=None, k_next=None):
        piece = half(xx, c, part)
        arrived(piece, rx.at[k], sx.at[k])
        if device is not None:
            send(piece, piece, sx.at[k_next], rx.at[k_next], device)
        send(piece, piece, sd.at[k], rd.at[k], d_core)

    def from_core(k, xx, part):
        arrived(half(xx, 1 - c, part), rd.at[k], sd.at[k])

    gq = gain[0:1, :] * QSCALE
    gk = gain[1:2, :]

    def project(k, d):
        rows = pl.ds(mo(d * CH, CH), CH)
        kv_rows = pl.ds(mo(OWN + d * CH, CH), CH)
        merged = jnp.dot(G[rows, :], WQ[...], preferred_element_type=F32)
        for g, gains in enumerate((gq, gk)):
            for h in range(HL):
                v = merged[:, g * W + h * HD: g * W + (h + 1) * HD]
                factor = lax.rsqrt(jnp.mean(v * v, axis=1, keepdims=True) + 1e-6)
                v = (v * factor * gains[:, h * HD:(h + 1) * HD]).astype(BF16)
                if g == 0:
                    Q[rows, h * HD:(h + 1) * HD] = v
                else:
                    KV[kv_rows, h * HD:(h + 1) * HD] = v
        KV[kv_rows, W:] = merged[:, 2 * W:].astype(BF16)
        frame = d // 2
        there = KV.at[pl.ds(mo((1 - frame) * HI + (d - 2 * frame) * CH, CH), CH)]
        send(KV.at[kv_rows], there, sn.at[k], rn.at[k], d_tm(2 * frame - 1))

    def far_slot(frame, level):
        if level == 4:
            return KV.at[pl.ds(FAR4, TB)]
        return KV.at[pl.ds(mo(FAR + frame * 3 * TB + (level - 1) * TB, TB), TB)]

    def chosen(base, n, first):
        at = [KV[pl.ds(mo(base + i * TB, TB), n), :] for i in range(3)]
        return jnp.where(first == 0, at[0], jnp.where(first == 1, at[1], at[2]))

    def send_far(frame, level, k, moved_by):
        asking = ((tm + moved_by + N_TM) % N_TM) * 2 + frame
        FS[k] = chosen(OWN + frame * 512, TB, band[asking, level])
        copy = remote(FS.at[k], far_slot(frame, level), sf.at[k], rf.at[k], d_tm(moved_by))
        copy.start()
        return copy

    def send_far_frame(frame, half_at):
        for level in (3, 2, 1):
            sign = 2 * ((level + frame) % 2) - 1
            sent.append(send_far(frame, level, 3 * half_at + level - 1, sign * 2 ** level))

    frame4 = 1 - tm // 16
    mine = x // 2

    loads[0].wait()
    for load in loads[1:4]:
        load.wait()
    arrived(G.at[pl.ds(mo((x * 2 + 1 - c) * TB, TB), TB)], rd.at[6], sd.at[6])
    project(0, x)

    pass_on(0, left, 0, d_right, 4)
    pass_on(2, right, 1, d_left, 5)
    pass_on(1, left, 1)
    pass_on(3, right, 0)
    for k, xx, part in ((0, left, 0), (1, left, 1), (2, right, 1), (3, right, 0)):
        from_core(k, xx, part)
    near_first = x + 1 - 2 * (x % 2)
    project(1, near_first)
    @pl.when(frame4 == mine)
    def _():
        send_far(mine, 4, 6, 16)

    send_far_frame(mine, 0)
    project(2, (near_first + 2) % 4)
    pass_on(4, across, 0)
    pass_on(5, across, 1)
    from_core(4, across, 0)
    from_core(5, across, 1)
    project(3, across)

    @pl.when(frame4 != mine)
    def _():
        send_far(1 - mine, 4, 6, 16)

    send_far_frame(1 - mine, 1)

    for k in range(4):
        d = (x, near_first, (near_first + 2) % 4, across)[k]
        frame = d // 2
        arrived(KV.at[pl.ds(mo((1 - frame) * HI + (d - 2 * frame) * CH, CH), CH)], rn.at[k], sn.at[k])

    def score_tiles(rows, lanes, tiles):
        q = Q[rows, lanes]
        top = None
        for t, (first, valid) in enumerate(tiles):
            keys = KV[pl.ds(first, KB), lanes]
            s = lax.dot_general(q, keys, (((1,), (1,)), ((), ())), preferred_element_type=F32)
            if valid is not None:
                s = jnp.where(valid, s, NEG)
            S[:, t * KB:(t + 1) * KB] = s
            both = jnp.maximum(s[:, :HD], s[:, HD:])
            top = both if top is None else jnp.maximum(top, both)
        return top

    def weigh_tiles(tiles, lanes_v, m):
        total = None
        acc = None
        for t, (first, _) in enumerate(tiles):
            p = jnp.exp2(S[:, t * KB:(t + 1) * KB] - m)
            both = p[:, :HD] + p[:, HD:]
            total = both if total is None else total + both
            part = jnp.dot(p.astype(BF16), KV[pl.ds(first, KB), lanes_v], preferred_element_type=F32)
            acc = part if acc is None else acc + part
        return total, acc

    for frame in range(2):
        KV[BAND0 + frame * KB:BAND0 + (frame + 1) * KB, :] = chosen((1 - frame) * HI, KB, band[tm * 2 + frame, 0])

    below = tm > 0
    above = tm < N_TM - 1

    @pl.loop(0, 4)
    def _(d):
        frame = d // 2
        rows = pl.ds(mo(d * CH, CH), CH)
        near_ok = jnp.logical_or(jnp.logical_and(frame == 0, below), jnp.logical_and(frame == 1, above))
        band_ok = jnp.logical_or(jnp.logical_and(frame == 1, below), jnp.logical_and(frame == 0, above))
        tiles = [(OWN + i * KB, None) for i in range(4)]
        tiles += [(mo(frame * HI + i * KB, KB), near_ok) for i in range(2)]
        tiles += [(mo(BAND0 + frame * KB, TB), band_ok)]
        for h in range(HL):
            lanes = slice(h * HD, (h + 1) * HD)
            top = score_tiles(rows, lanes, tiles)
            m = jnp.broadcast_to(jnp.max(top, axis=1, keepdims=True), (CH, HD))
            total, acc = weigh_tiles(tiles, slice(W + h * HD, W + (h + 1) * HD), m[:, :1])
            MX[rows, lanes] = m
            LS[rows, lanes] = total
            ACC[rows, lanes] = acc

    for half_at in range(2):
        frame = mine if half_at == 0 else 1 - mine
        for level in (3, 2, 1):
            k = 3 * half_at + level - 1
            arrived(far_slot(frame, level), rf.at[k], sf.at[k])
    arrived(far_slot(0, 4), rf.at[6], sf.at[6])
    loads[4].wait()
    arrived(WO.at[pl.ds(W, W)], rd.at[7], sd.at[7])

    def far_ok(frame, level):
        other = tm + (1 - 2 * ((frame + level) % 2)) * 2 ** level
        return jnp.logical_and(other >= 0, other < N_TM)

    def finish(step, d):
        frame = d // 2
        rows = pl.ds(mo(d * CH, CH), CH)
        segs = [(mo(FAR + frame * 3 * TB + (level - 1) * TB, TB), far_ok(frame, level)) for level in (1, 2, 3)]
        segs.append((FAR4, far_ok(frame, 4)))
        for h in range(HL):
            lanes = slice(h * HD, (h + 1) * HD)
            lanes_v = slice(W + h * HD, W + (h + 1) * HD)
            q = Q[rows, lanes]
            m_old = MX[rows, lanes]
            scores = []
            top = None
            for first, valid in segs:
                s = lax.dot_general(q, KV[pl.ds(first, TB), lanes], (((1,), (1,)), ((), ())),
                                    preferred_element_type=F32)
                s = jnp.where(valid, s, NEG)
                scores.append(s)
                top = s if top is None else jnp.maximum(top, s)
            m = jnp.maximum(m_old, jnp.max(top, axis=1, keepdims=True))
            scale = jnp.exp2(m_old - m)
            total = LS[rows, lanes] * scale
            acc = ACC[rows, lanes] * scale
            for s, (first, _) in zip(scores, segs):
                p = jnp.exp2(s - m)
                total = total + p
                acc = acc + jnp.dot(p.astype(BF16), KV[pl.ds(first, TB), lanes_v], preferred_element_type=F32)
            AF[step, :, lanes] = (acc / jnp.sum(total, axis=1, keepdims=True)).astype(BF16)
        send(AF.at[step, pl.ds(mo((1 - c) * TB, TB), TB)], A2.at[step, :, pl.ds(W, W)],
             sa.at[step], ra.at[step], d_core)
        A2[step, :, :W] = AF[step, pl.ds(mo(c * TB, TB), TB), :]
        arrived(A2.at[step, :, pl.ds(W, W)], ra.at[step], sa.at[step])

    NB = 512

    def product(step, lo, n, cols):
        return jnp.dot(A2[step, lo:lo + n, :], WO[:, cols], preferred_element_type=F32)

    columns = [slice(i * NB, (i + 1) * NB) for i in range(D // NB)]

    finish(0, across)
    for cols in columns:
        P0[:, cols] = product(0, 0, TB, cols).astype(BF16)
    send(P0.at[pl.ds(0, H)], RU, sr.at[0], rr.at[0], d_right)
    send(P0.at[pl.ds(H, H)], RD, sr.at[1], rr.at[1], d_left)

    finish(1, right)
    for cols in columns:
        P1[:, cols] = product(1, 0, TB, cols).astype(BF16)
    send(P1.at[pl.ds(H, H)], RL.at[pl.ds(H, H)], sr.at[2], rr.at[2], d_right)
    finish(2, left)
    for cols in columns:
        P2[:, cols] = product(2, 0, TB, cols).astype(BF16)
    send(P2.at[pl.ds(0, H)], RR.at[pl.ds(0, H)], sr.at[3], rr.at[3], d_left)

    arrived(RU, rr.at[0], sr.at[0])
    P1[0:H, :] = (P1[0:H, :].astype(F32) + RU[...].astype(F32)).astype(BF16)
    send(P1.at[pl.ds(0, H)], RL.at[pl.ds(0, H)], sr.at[4], rr.at[4], d_right)
    arrived(RD, rr.at[1], sr.at[1])
    P2[H:, :] = (P2[H:, :].astype(F32) + RD[...].astype(F32)).astype(BF16)
    send(P2.at[pl.ds(H, H)], RR.at[pl.ds(H, H)], sr.at[5], rr.at[5], d_left)

    finish(3, x)
    for cols in columns:
        P3[:, cols] = product(3, 0, TB, cols)
    arrived(RL.at[pl.ds(H, H)], rr.at[2], sr.at[2])
    arrived(RR.at[pl.ds(0, H)], rr.at[3], sr.at[3])
    arrived(RL.at[pl.ds(0, H)], rr.at[4], sr.at[4])
    arrived(RR.at[pl.ds(H, H)], rr.at[5], sr.at[5])
    out[...] = (P3[...] + RL[...].astype(F32) + RR[...].astype(F32)).astype(BF16)

    for copy in sent:
        copy.wait_send()
    remote(FS.at[6], far_slot(0, 4), sf.at[6], rf.at[6], d_tm(16)).wait_send()


def shards(tokens, w_qkv, qk_gain, w_out, band_start):
    w3 = jnp.transpose(w_qkv, (1, 0, 2))
    vmem = pl.BlockSpec(memory_space=pltpu.VMEM)
    hbm = pl.BlockSpec(memory_space=pl.ANY)
    dma = pltpu.SemaphoreType.DMA
    return pl.pallas_call(
        kernel,
        out_shape=jax.ShapeDtypeStruct((TB, D), BF16),
        in_specs=[hbm, hbm, vmem, hbm, pl.BlockSpec(memory_space=pltpu.SMEM)],
        out_specs=vmem,
        scratch_shapes=[
            pltpu.VMEM((ROWS, D), BF16),
            pltpu.VMEM((D, 3 * W), BF16),
            pltpu.VMEM((2 * W, D), BF16),
            pltpu.VMEM((ROWS, W), BF16),
            pltpu.VMEM((KV_ROWS, 2 * W), BF16),
            pltpu.VMEM((7, TB, 2 * W), BF16),
            pltpu.VMEM((ROWS, W), F32),
            pltpu.VMEM((ROWS, W), F32),
            pltpu.VMEM((ROWS, W), F32),
            pltpu.VMEM((CH, 7 * KB), F32),
            pltpu.VMEM((16, 128), BF16),
            pltpu.VMEM((4, CH, W), BF16),
            pltpu.VMEM((4, TB, 2 * W), BF16),
            pltpu.VMEM((TB, D), BF16),
            pltpu.VMEM((TB, D), BF16),
            pltpu.VMEM((TB, D), BF16),
            pltpu.VMEM((TB, D), F32),
            pltpu.VMEM((TB // 2, D), BF16),
            pltpu.VMEM((TB // 2, D), BF16),
            pltpu.VMEM((TB, D), BF16),
            pltpu.VMEM((TB, D), BF16),
            dma((5,)), dma((6,)), dma((6,)), dma((8,)), dma((8,)), dma((4,)), dma((4,)),
            dma((7,)), dma((7,)), dma((4,)), dma((4,)), dma((6,)), dma((6,)),
        ],
        compiler_params=pltpu.CompilerParams(
            collective_id=0, has_side_effects=True, vmem_limit_bytes=60 * 2**20),
        cost_estimate=pl.CostEstimate(flops=14 * 10**9, bytes_accessed=12 * 10**6, transcendentals=7 * 10**6),
        name="band_attention",
    )(tokens, w3, qk_gain, w_out, band_start)


def solution(mesh):
    placed = (P(("tm", "row"), None), P(None, None, "row"), P(None, "row"), P("row", None), P())
    return jax.shard_map(
        shards, mesh=mesh, in_specs=placed, out_specs=P(("tm", "row"), None), check_vma=False
    )
```

```python
import functools
import math

import jax
import jax.numpy as jnp
from jax import lax
from jax.experimental import pallas as pl
from jax.experimental.pallas import tpu as pltpu
from jax.sharding import PartitionSpec as P

MESH = pl.DeviceIdType.MESH
D = 3072
HD = 128
HL = 3
W = HL * HD
TB = 128
CH = 2 * TB
ROWS = 4 * CH
N_TM = 32
LO, OWN, HI, FAR, FAR4, BAND0 = 0, 512, 1536, 2048, 2816, 2944
KV_ROWS = 3456
QSCALE = math.log2(math.e) / math.sqrt(HD)
NEG = -1e30
KB = 256
F32 = jnp.float32
BF16 = jnp.bfloat16


def mo(value, by):
    return pl.multiple_of(value, by)


def kernel(
    tok, w3, gain, wout, band, out,
    G, GH, WQ, WO, Q, KV, FS, ACC, MX, LS, S, AF, A2, P0, P1, P2, P3, RU, RD, RL, RR,
    loc, sx, rx, sd, rd, sn, rn, sf, rf, sa, ra, sr, rr,
):
    tm = lax.axis_index("tm")
    row = lax.axis_index("row")
    x = row // 2
    c = row % 2
    right = (x + 1) % 4
    left = (x + 3) % 4
    across = (x + 2) % 4
    d_right = (tm, right * 2 + c)
    d_left = (tm, left * 2 + c)
    d_core = (tm, x * 2 + (1 - c))

    def d_tm(shift):
        return ((tm + shift + N_TM) % N_TM, row)

    loads = [pltpu.make_async_copy(tok, G.at[pl.ds(mo(row * TB, TB), TB)], loc.at[0])]
    for j in range(3):
        loads.append(pltpu.make_async_copy(w3.at[j], WQ.at[:, pl.ds(j * W, W)], loc.at[1 + j]))
    loads.append(pltpu.make_async_copy(wout, WO.at[pl.ds(0, W)], loc.at[4]))
    for load in loads:
        load.start()

    partners = [d_right, d_left, d_core, d_tm(1), d_tm(-1), d_tm(2), d_tm(-2),
                d_tm(4), d_tm(-4), d_tm(8), d_tm(-8), d_tm(16)]
    barrier = pltpu.get_barrier_semaphore()
    for device in partners:
        pl.semaphore_signal(barrier, inc=1, device_id=device, device_id_type=MESH)
    loads[0].wait()
    pl.semaphore_wait(barrier, len(partners))

    def remote(src, dst, send, recv, device):
        return pltpu.make_async_remote_copy(
            src_ref=src, dst_ref=dst, send_sem=send, recv_sem=recv,
            device_id=device, device_id_type=MESH)

    sent = []

    def send(src, dst, send_sem, recv_sem, device):
        copy = remote(src, dst, send_sem, recv_sem, device)
        copy.start()
        sent.append(copy)

    def arrived(dst, recv_sem, send_sem):
        remote(dst, dst, send_sem, recv_sem, d_core).wait_recv()

    H = TB // 2

    def gather(G, base):
        def block(xx, cc):
            return G.at[pl.ds(mo((xx * 2 + cc) * TB, TB), TB)]

        def half(xx, part, cc=c):
            return G.at[pl.ds(mo(((xx * 2 + cc) * 2 + part) * H, H), H)]

        def pass_on(k, xx, part, device=None, k_next=None):
            piece = half(xx, part)
            arrived(piece, rx.at[base + k], sx.at[base + k])
            if device is not None:
                send(piece, piece, sx.at[base + k_next], rx.at[base + k_next], device)
            send(piece, piece, sd.at[base + k], rd.at[base + k], d_core)

        def from_core(k, xx, part):
            arrived(half(xx, part, 1 - c), rd.at[base + k], sd.at[base + k])

        def begin():
            send(half(x, 0), half(x, 0), sx.at[base], rx.at[base], d_right)
            send(half(x, 1), half(x, 1), sx.at[base + 2], rx.at[base + 2], d_left)
            send(block(x, c), block(x, c), sd.at[base + 6], rd.at[base + 6], d_core)
            send(half(x, 1), half(x, 1), sx.at[base + 1], rx.at[base + 1], d_right)
            send(half(x, 0), half(x, 0), sx.at[base + 3], rx.at[base + 3], d_left)

        def first():
            arrived(block(x, 1 - c), rd.at[base + 6], sd.at[base + 6])

        def middle():
            pass_on(0, left, 0, d_right, 4)
            pass_on(2, right, 1, d_left, 5)
            pass_on(1, left, 1)
            pass_on(3, right, 0)
            for k, xx, part in ((0, left, 0), (1, left, 1), (2, right, 1), (3, right, 0)):
                from_core(k, xx, part)

        def last():
            pass_on(4, across, 0)
            pass_on(5, across, 1)
            from_core(4, across, 0)
            from_core(5, across, 1)

        return begin, first, middle, last

    own = G.at[pl.ds(mo(row * TB, TB), TB)]
    begin, first, middle, last = gather(G, 0)
    begin_halo, first_halo, middle_halo, last_halo = gather(GH, 7)
    begin()
    own_halo = GH.at[pl.ds(mo(row * TB, TB), TB)]
    send(own, own_halo, sn.at[0], rn.at[0], d_tm(2 * (x // 2) - 1))

    gq = gain[0:1, :] * QSCALE
    gk = gain[1:2, :]

    def normed(v, gains):
        factor = lax.rsqrt(jnp.mean(v * v, axis=1, keepdims=True) + 1e-6)
        return (v * factor * gains).astype(BF16)

    def project(tokens, first_row, d):
        merged = jnp.dot(tokens[pl.ds(mo(d * CH, CH), CH), :], WQ[:, W:], preferred_element_type=F32)
        rows = pl.ds(mo(first_row, CH), CH)
        for h in range(HL):
            lanes = slice(h * HD, (h + 1) * HD)
            KV[rows, lanes] = normed(merged[:, lanes], gk[:, lanes])
        KV[rows, W:] = merged[:, W:].astype(BF16)

    def project_own(d):
        project(G, OWN + d * CH, d)

    def project_halo(d):
        frame = d // 2
        project(GH, (1 - frame) * HI + (d - 2 * frame) * CH, d)

    def far_slot(frame, level):
        if level == 4:
            return KV.at[pl.ds(FAR4, TB)]
        return KV.at[pl.ds(mo(FAR + frame * 3 * TB + (level - 1) * TB, TB), TB)]

    def chosen(base, n, first):
        at = [KV[pl.ds(mo(base + i * TB, TB), n), :] for i in range(3)]
        return jnp.where(first == 0, at[0], jnp.where(first == 1, at[1], at[2]))

    def send_far(frame, level, k, moved_by):
        asking = ((tm + moved_by + N_TM) % N_TM) * 2 + frame
        FS[k] = chosen(OWN + frame * 512, TB, band[level, asking])
        copy = remote(FS.at[k], far_slot(frame, level), sf.at[k], rf.at[k], d_tm(moved_by))
        copy.start()
        return copy

    def send_far_frame(frame, half_at):
        for level in (1, 2, 3):
            sign = 2 * ((level + frame) % 2) - 1
            sent.append(send_far(frame, level, 3 * half_at + level - 1, sign * 2 ** level))

    frame4 = 1 - tm // 16
    mine = x // 2

    for load in loads[2:4]:
        load.wait()
    first()
    project_own(x)
    middle()
    near_first = x + 1 - 2 * (x % 2)
    near_other = (near_first + 2) % 4
    project_own(near_first)

    @pl.when(frame4 == mine)
    def _():
        send_far(mine, 4, 6, 16)

    send_far_frame(mine, 0)
    project_own(near_other)
    arrived(own_halo, rn.at[0], sn.at[0])
    begin_halo()
    last()
    project_own(across)

    @pl.when(frame4 != mine)
    def _():
        send_far(1 - mine, 4, 6, 16)

    send_far_frame(1 - mine, 1)
    loads[4].wait()
    send(WO.at[pl.ds(0, W)], WO.at[pl.ds(W, W)], sd.at[14], rd.at[14], d_core)

    loads[1].wait()

    @pl.loop(0, 2)
    def _(i):
        rows = pl.ds(mo(i * 512, 512), 512)
        merged = jnp.dot(G[rows, :], WQ[:, :W], preferred_element_type=F32)
        for h in range(HL):
            lanes = slice(h * HD, (h + 1) * HD)
            Q[rows, lanes] = normed(merged[:, lanes], gq[:, lanes])

    def score_tiles(rows, lanes, tiles, top=None):
        q = Q[rows, lanes]
        at = 0
        for begins, n, valid in tiles:
            s = lax.dot_general(q, KV[pl.ds(begins, n), lanes], (((1,), (1,)), ((), ())), preferred_element_type=F32)
            if valid is not None:
                s = jnp.where(valid, s, NEG)
            S[:, at:at + n] = s
            at += n
            for i in range(0, n, HD):
                top = s[:, i:i + HD] if top is None else jnp.maximum(top, s[:, i:i + HD])
        return top

    def weigh_tiles(tiles, lanes_v, m, total=None, acc=None):
        at = 0
        for begins, n, _ in tiles:
            p = jnp.exp2(S[:, at:at + n] - m)
            at += n
            for i in range(0, n, HD):
                total = p[:, i:i + HD] if total is None else total + p[:, i:i + HD]
            part = jnp.dot(p.astype(BF16), KV[pl.ds(begins, n), lanes_v], preferred_element_type=F32)
            acc = part if acc is None else acc + part
        return total, acc

    @pl.loop(0, 4)
    def _(d):
        rows = pl.ds(mo(d * CH, CH), CH)
        tiles = [(OWN + i * KB, KB, None) for i in range(4)]
        for h in range(HL):
            lanes = slice(h * HD, (h + 1) * HD)
            top = score_tiles(rows, lanes, tiles)
            m = jnp.broadcast_to(jnp.max(top, axis=1, keepdims=True), (CH, HD))
            total, acc = weigh_tiles(tiles, slice(W + h * HD, W + (h + 1) * HD), m[:, :1])
            MX[rows, lanes] = m
            LS[rows, lanes] = total
            ACC[rows, lanes] = acc

    first_halo()
    project_halo(x)
    middle_halo()
    project_halo(near_first)
    project_halo(near_other)
    last_halo()
    project_halo(across)
    for frame in range(2):
        KV[BAND0 + frame * KB:BAND0 + (frame + 1) * KB, :] = chosen((1 - frame) * HI, KB, band[0, tm * 2 + frame])

    for half_at in range(2):
        frame = mine if half_at == 0 else 1 - mine
        for level in (3, 2, 1):
            k = 3 * half_at + level - 1
            arrived(far_slot(frame, level), rf.at[k], sf.at[k])
    arrived(far_slot(0, 4), rf.at[6], sf.at[6])
    arrived(WO.at[pl.ds(W, W)], rd.at[14], sd.at[14])

    def far_ok(frame, level):
        other = tm + (1 - 2 * ((frame + level) % 2)) * 2 ** level
        return jnp.logical_and(other >= 0, other < N_TM)

    def near_ok(frame):
        other = tm + 2 * frame - 1
        return jnp.logical_and(other >= 0, other < N_TM)

    def finish(step, d):
        frame = d // 2
        rows = pl.ds(mo(d * CH, CH), CH)
        tiles = [(mo(frame * HI + i * KB, KB), KB, near_ok(frame)) for i in range(2)]
        tiles += [(mo(BAND0 + frame * KB, TB), KB, near_ok(1 - frame))]
        tiles += [(mo(FAR + frame * 3 * TB + (level - 1) * TB, TB), TB, far_ok(frame, level)) for level in (1, 2, 3)]
        tiles += [(FAR4, TB, far_ok(frame, 4))]
        for h in range(HL):
            lanes = slice(h * HD, (h + 1) * HD)
            lanes_v = slice(W + h * HD, W + (h + 1) * HD)
            top = score_tiles(rows, lanes, tiles)
            m_old = MX[rows, lanes]
            m = jnp.maximum(m_old, jnp.max(top, axis=1, keepdims=True))
            scale = jnp.exp2(m_old - m)
            total, acc = weigh_tiles(tiles, lanes_v, m[:, :1], LS[rows, lanes] * scale, ACC[rows, lanes] * scale)
            AF[step, :, lanes] = (acc / jnp.sum(total, axis=1, keepdims=True)).astype(BF16)
        send(AF.at[step, pl.ds(mo((1 - c) * TB, TB), TB)], A2.at[step, :, pl.ds(W, W)],
             sa.at[step], ra.at[step], d_core)
        A2[step, :, :W] = AF[step, pl.ds(mo(c * TB, TB), TB), :]
        arrived(A2.at[step, :, pl.ds(W, W)], ra.at[step], sa.at[step])

    NB = 512

    def product(step, lo, n, cols):
        return jnp.dot(A2[step, lo:lo + n, :], WO[:, cols], preferred_element_type=F32)

    columns = [slice(i * NB, (i + 1) * NB) for i in range(D // NB)]

    finish(0, across)
    for cols in columns:
        P0[:, cols] = product(0, 0, TB, cols).astype(BF16)
    send(P0.at[pl.ds(0, H)], RU, sr.at[0], rr.at[0], d_right)
    send(P0.at[pl.ds(H, H)], RD, sr.at[1], rr.at[1], d_left)

    finish(1, right)
    for cols in columns:
        P1[:, cols] = product(1, 0, TB, cols).astype(BF16)
    send(P1.at[pl.ds(H, H)], RL.at[pl.ds(H, H)], sr.at[2], rr.at[2], d_right)
    finish(2, left)
    for cols in columns:
        P2[:, cols] = product(2, 0, TB, cols).astype(BF16)
    send(P2.at[pl.ds(0, H)], RR.at[pl.ds(0, H)], sr.at[3], rr.at[3], d_left)

    arrived(RU, rr.at[0], sr.at[0])
    P1[0:H, :] = (P1[0:H, :].astype(F32) + RU[...].astype(F32)).astype(BF16)
    send(P1.at[pl.ds(0, H)], RL.at[pl.ds(0, H)], sr.at[4], rr.at[4], d_right)
    arrived(RD, rr.at[1], sr.at[1])
    P2[H:, :] = (P2[H:, :].astype(F32) + RD[...].astype(F32)).astype(BF16)
    send(P2.at[pl.ds(H, H)], RR.at[pl.ds(H, H)], sr.at[5], rr.at[5], d_left)

    finish(3, x)
    for cols in columns:
        P3[:, cols] = product(3, 0, TB, cols)
    arrived(RL.at[pl.ds(H, H)], rr.at[2], sr.at[2])
    arrived(RR.at[pl.ds(0, H)], rr.at[3], sr.at[3])
    arrived(RL.at[pl.ds(0, H)], rr.at[4], sr.at[4])
    arrived(RR.at[pl.ds(H, H)], rr.at[5], sr.at[5])
    out[...] = (P3[...] + RL[...].astype(F32) + RR[...].astype(F32)).astype(BF16)

    for copy in sent:
        copy.wait_send()
    remote(FS.at[6], far_slot(0, 4), sf.at[6], rf.at[6], d_tm(16)).wait_send()


def shards(tokens, w_qkv, qk_gain, w_out, band_start):
    w3 = jnp.transpose(w_qkv, (1, 0, 2))
    vmem = pl.BlockSpec(memory_space=pltpu.VMEM)
    hbm = pl.BlockSpec(memory_space=pl.ANY)
    dma = pltpu.SemaphoreType.DMA
    return pl.pallas_call(
        kernel,
        out_shape=jax.ShapeDtypeStruct((TB, D), BF16),
        in_specs=[hbm, hbm, vmem, hbm, pl.BlockSpec(memory_space=pltpu.SMEM)],
        out_specs=vmem,
        scratch_shapes=[
            pltpu.VMEM((ROWS, D), BF16),
            pltpu.VMEM((ROWS, D), BF16),
            pltpu.VMEM((D, 3 * W), BF16),
            pltpu.VMEM((2 * W, D), BF16),
            pltpu.VMEM((ROWS, W), BF16),
            pltpu.VMEM((KV_ROWS, 2 * W), BF16),
            pltpu.VMEM((7, TB, 2 * W), BF16),
            pltpu.VMEM((ROWS, W), F32),
            pltpu.VMEM((ROWS, W), F32),
            pltpu.VMEM((ROWS, W), F32),
            pltpu.VMEM((CH, 5 * KB), F32),
            pltpu.VMEM((4, CH, W), BF16),
            pltpu.VMEM((4, TB, 2 * W), BF16),
            pltpu.VMEM((TB, D), BF16),
            pltpu.VMEM((TB, D), BF16),
            pltpu.VMEM((TB, D), BF16),
            pltpu.VMEM((TB, D), F32),
            pltpu.VMEM((TB // 2, D), BF16),
            pltpu.VMEM((TB // 2, D), BF16),
            pltpu.VMEM((TB, D), BF16),
            pltpu.VMEM((TB, D), BF16),
            dma((5,)), dma((13,)), dma((13,)), dma((15,)), dma((15,)), dma((1,)), dma((1,)),
            dma((7,)), dma((7,)), dma((4,)), dma((4,)), dma((6,)), dma((6,)),
        ],
        compiler_params=pltpu.CompilerParams(
            collective_id=0, has_side_effects=True, vmem_limit_bytes=60 * 2**20),
        cost_estimate=pl.CostEstimate(flops=14 * 10**9, bytes_accessed=12 * 10**6, transcendentals=7 * 10**6),
        name="band_attention",
    )(tokens, w3, qk_gain, w_out, jnp.transpose(band_start))


def solution(mesh):
    placed = (P(("tm", "row"), None), P(None, None, "row"), P(None, "row"), P("row", None), P())
    return jax.shard_map(
        shards, mesh=mesh, in_specs=placed, out_specs=P(("tm", "row"), None), check_vma=False
    )
```

```python
import functools
import math

import jax
import jax.numpy as jnp
from jax import lax
from jax.experimental import pallas as pl
from jax.experimental.pallas import tpu as pltpu
from jax.sharding import PartitionSpec as P

MESH = pl.DeviceIdType.MESH
D = 3072
HD = 128
HL = 3
W = HL * HD
TB = 128
CH = 2 * TB
ROWS = 4 * CH
N_TM = 32
LO, OWN, HI, FAR, FAR4, BAND0 = 0, 512, 1536, 2048, 2816, 2944
KV_ROWS = 3456
QSCALE = math.log2(math.e) / math.sqrt(HD)
NEG = -1e30
NR = 96
KB = 256
F32 = jnp.float32
BF16 = jnp.bfloat16


def mo(value, by):
    return pl.multiple_of(value, by)


def kernel(
    tok, w3, gain, wout, band, out,
    G, GH, WQ, WO, Q, KV, FS, ACC, MX, LS, S, AF, A2, P0, P1, P2, P3, RU, RD, RL, RR,
    loc, sx, rx, sd, rd, sn, rn, sf, rf, sa, ra, sr, rr, known,
):
    tm = lax.axis_index("tm")
    row = lax.axis_index("row")
    x = row // 2
    c = row % 2
    right = (x + 1) % 4
    left = (x + 3) % 4
    across = (x + 2) % 4
    d_right = (tm, right * 2 + c)
    d_left = (tm, left * 2 + c)
    d_core = (tm, x * 2 + (1 - c))

    def d_tm(shift):
        return ((tm + shift + N_TM) % N_TM, row)

    loads = [pltpu.make_async_copy(tok, G.at[pl.ds(mo(row * TB, TB), TB)], loc.at[0])]
    for j in range(3):
        loads.append(pltpu.make_async_copy(w3.at[j], WQ.at[:, pl.ds(j * W, W)], loc.at[1 + j]))
    loads.append(pltpu.make_async_copy(wout, WO.at[pl.ds(0, W)], loc.at[4]))
    for load in loads:
        load.start()

    def signal(semaphore, device):
        pl.semaphore_signal(semaphore, inc=1, device_id=device, device_id_type=MESH)

    KV[FAR:, W:] = jnp.zeros((KV_ROWS - FAR, W), BF16)
    for block in range(4):
        for first in (LO, HI):
            KV[first + block * TB + NR:first + (block + 1) * TB, W:] = jnp.zeros((TB - NR, W), BF16)

    def inside(shift):
        return jnp.logical_and(tm + shift >= 0, tm + shift < N_TM)

    def count(*shifts):
        total = 0
        for shift in shifts:
            total = total + inside(shift).astype(jnp.int32)
        return total

    barrier = pltpu.get_barrier_semaphore()
    for device in (d_right, d_left, d_core):
        signal(barrier, device)

    def signal_tm(semaphore, shift):
        @pl.when(inside(shift))
        def _():
            signal(semaphore, d_tm(shift))

    signal_tm(barrier, 1)
    signal_tm(barrier, -1)
    loads[0].wait()
    pl.semaphore_wait(barrier, 3 + count(1, -1))

    def tell(level):
        signal_tm(known.at[level], 2 ** level)
        signal_tm(known.at[level], -(2 ** level))

    def heard(level):
        pl.semaphore_wait(known.at[level], count(2 ** level, -(2 ** level)))

    def remote(src, dst, send, recv, device):
        return pltpu.make_async_remote_copy(
            src_ref=src, dst_ref=dst, send_sem=send, recv_sem=recv,
            device_id=device, device_id_type=MESH)

    sent = []

    def send(src, dst, send_sem, recv_sem, device):
        copy = remote(src, dst, send_sem, recv_sem, device)
        copy.start()
        sent.append(copy)

    sent_if = []

    def send_if(here, src, dst, send_sem, recv_sem, device):
        copy = remote(src, dst, send_sem, recv_sem, device)

        @pl.when(here)
        def _():
            copy.start()

        sent_if.append((here, copy))

    def arrived_if(here, dst, recv_sem, send_sem):
        @pl.when(here)
        def _():
            arrived(dst, recv_sem, send_sem)

    def arrived(dst, recv_sem, send_sem):
        remote(dst, dst, send_sem, recv_sem, d_core).wait_recv()

    H = TB // 2

    def gather(G, n, base):
        H = n // 2

        def block(xx, cc):
            return G.at[pl.ds(mo((xx * 2 + cc) * n, n), n)]

        def half(xx, part, cc=c):
            return G.at[pl.ds(mo(((xx * 2 + cc) * 2 + part) * H, H), H)]

        def pass_on(k, xx, part, device=None, k_next=None):
            piece = half(xx, part)
            arrived(piece, rx.at[base + k], sx.at[base + k])
            if device is not None:
                send(piece, piece, sx.at[base + k_next], rx.at[base + k_next], device)
            send(piece, piece, sd.at[base + k], rd.at[base + k], d_core)

        def from_core(k, xx, part):
            arrived(half(xx, part, 1 - c), rd.at[base + k], sd.at[base + k])

        def begin():
            send(half(x, 0), half(x, 0), sx.at[base], rx.at[base], d_right)
            send(half(x, 1), half(x, 1), sx.at[base + 2], rx.at[base + 2], d_left)
            send(block(x, c), block(x, c), sd.at[base + 6], rd.at[base + 6], d_core)
            send(half(x, 1), half(x, 1), sx.at[base + 1], rx.at[base + 1], d_right)
            send(half(x, 0), half(x, 0), sx.at[base + 3], rx.at[base + 3], d_left)

        def first():
            arrived(block(x, 1 - c), rd.at[base + 6], sd.at[base + 6])

        def middle():
            pass_on(0, left, 0, d_right, 4)
            pass_on(2, right, 1, d_left, 5)
            pass_on(1, left, 1)
            pass_on(3, right, 0)
            for k, xx, part in ((0, left, 0), (1, left, 1), (2, right, 1), (3, right, 0)):
                from_core(k, xx, part)

        def last():
            pass_on(4, across, 0)
            pass_on(5, across, 1)
            from_core(4, across, 0)
            from_core(5, across, 1)

        return begin, first, middle, last

    own = G.at[pl.ds(mo(row * TB, TB), TB)]
    begin, first, middle, last = gather(G, TB, 0)
    begin_halo, first_halo, middle_halo, last_halo = gather(GH, NR, 7)
    begin()
    tell(0)
    own_halo = GH.at[pl.ds(mo(row * NR, NR), NR)]
    own_part = G.at[pl.ds(mo(row * TB, TB), NR)]
    up = 2 * (x // 2) - 1
    send_if(inside(up), own_part, own_halo, sn.at[0], rn.at[0], d_tm(up))

    @pl.when(jnp.logical_not(inside(-up)))
    def _():
        filler = pltpu.make_async_copy(own_part, own_halo, loc.at[0])
        filler.start()
        filler.wait()


    gq = gain[0:1, :] * QSCALE
    gk = gain[1:2, :]

    def normed(v, gains):
        factor = lax.rsqrt(jnp.mean(v * v, axis=1, keepdims=True) + 1e-6)
        return (v * factor * gains).astype(BF16)

    def project(tokens, n, first_row):
        merged = jnp.dot(tokens, WQ[:, W:], preferred_element_type=F32)
        for cc in range(2):
            rows = pl.ds(mo(first_row + cc * TB, TB), n)
            mine = merged[cc * n:(cc + 1) * n]
            for h in range(HL):
                lanes = slice(h * HD, (h + 1) * HD)
                KV[rows, lanes] = normed(mine[:, lanes], gk[:, lanes])
            KV[rows, W:] = mine[:, W:].astype(BF16)

    def halo_row(d):
        frame = d // 2
        return (1 - frame) * HI + (d - 2 * frame) * CH

    def near_piece(d, cc):
        return KV.at[pl.ds(mo(halo_row(d) + cc * TB + NR, 16), TB - NR)]

    def project_own(k, d):
        project(G[pl.ds(mo(d * CH, CH), CH), :], TB, OWN + d * CH)
        for cc in range(2):
            to = 2 * (d // 2) - 1
            send_if(inside(to), KV.at[pl.ds(mo(OWN + d * CH + cc * TB + NR, 16), TB - NR)], near_piece(d, cc),
                    sn.at[1 + 2 * k + cc], rn.at[1 + 2 * k + cc], d_tm(to))

    def project_halo(d):
        project(GH[pl.ds(mo(d * 2 * NR, 2 * NR), 2 * NR), :], NR, halo_row(d))

    def far_slot(frame, level):
        if level == 4:
            return KV.at[pl.ds(FAR4, TB)]
        return KV.at[pl.ds(mo(FAR + frame * 3 * TB + (level - 1) * TB, TB), TB)]

    def chosen(base, n, first):
        at = [KV[pl.ds(mo(base + i * TB, TB), n), :] for i in range(3)]
        return jnp.where(first == 0, at[0], jnp.where(first == 1, at[1], at[2]))

    def stage_far(frame, level, k, moved_by):
        asking = ((tm + moved_by + N_TM) % N_TM) * 2 + frame
        FS[k] = chosen(OWN + frame * 512, TB, band[level, asking])

    def send_far(half_at, level):
        frame = mine if half_at == 0 else 1 - mine
        moved_by = (2 * ((level + frame) % 2) - 1) * 2 ** level
        k = 3 * half_at + level - 1
        stage_far(frame, level, k, moved_by)
        send_if(inside(moved_by), FS.at[k], far_slot(frame, level), sf.at[k], rf.at[k], d_tm(moved_by))

    frame4 = 1 - tm // 16
    mine = x // 2

    for load in loads[2:4]:
        load.wait()
    first()
    project_own(0, x)
    heard(0)
    tell(1)
    middle()
    heard(1)
    tell(2)
    near_first = x + 1 - 2 * (x % 2)
    near_other = (near_first + 2) % 4
    project_own(1, near_first)
    send_far(0, 2)
    send_far(0, 1)
    project_own(2, near_other)
    arrived_if(inside(-up), own_halo, rn.at[0], sn.at[0])
    begin_halo()
    heard(2)
    tell(3)
    send_far(0, 3)
    last()
    project_own(3, across)
    send_far(1, 3)
    heard(3)
    stage_far(frame4, 4, 6, 16)
    send(FS.at[6], far_slot(0, 4), sf.at[6], rf.at[6], d_tm(16))
    send_far(1, 2)
    send_far(1, 1)
    loads[4].wait()
    send(WO.at[pl.ds(0, W)], WO.at[pl.ds(W, W)], sd.at[14], rd.at[14], d_core)

    loads[1].wait()

    @pl.loop(0, 2)
    def _(i):
        rows = pl.ds(mo(i * 512, 512), 512)
        merged = jnp.dot(G[rows, :], WQ[:, :W], preferred_element_type=F32)
        for h in range(HL):
            lanes = slice(h * HD, (h + 1) * HD)
            Q[rows, lanes] = normed(merged[:, lanes], gq[:, lanes])

    def score_tiles(rows, lanes, tiles, top=None):
        q = Q[rows, lanes]
        at = 0
        for begins, n, valid in tiles:
            s = lax.dot_general(q, KV[pl.ds(begins, n), lanes], (((1,), (1,)), ((), ())), preferred_element_type=F32)
            if valid is not None:
                s = jnp.where(valid, s, NEG)
            S[:, at:at + n] = s
            at += n
            for i in range(0, n, HD):
                top = s[:, i:i + HD] if top is None else jnp.maximum(top, s[:, i:i + HD])
        return top

    def weigh_tiles(tiles, lanes_v, m, total=None, acc=None):
        at = 0
        for begins, n, _ in tiles:
            p = jnp.exp2(S[:, at:at + n] - m)
            at += n
            for i in range(0, n, HD):
                total = p[:, i:i + HD] if total is None else total + p[:, i:i + HD]
            part = jnp.dot(p.astype(BF16), KV[pl.ds(begins, n), lanes_v], preferred_element_type=F32)
            acc = part if acc is None else acc + part
        return total, acc

    @pl.loop(0, 4)
    def _(d):
        rows = pl.ds(mo(d * CH, CH), CH)
        tiles = [(OWN + i * KB, KB, None) for i in range(4)]
        for h in range(HL):
            lanes = slice(h * HD, (h + 1) * HD)
            top = score_tiles(rows, lanes, tiles)
            m = jnp.broadcast_to(jnp.max(top, axis=1, keepdims=True), (CH, HD))
            total, acc = weigh_tiles(tiles, slice(W + h * HD, W + (h + 1) * HD), m[:, :1])
            MX[rows, lanes] = m
            LS[rows, lanes] = total
            ACC[rows, lanes] = acc

    first_halo()
    project_halo(x)
    middle_halo()
    project_halo(near_first)
    project_halo(near_other)
    last_halo()
    project_halo(across)
    for k, d in enumerate((x, near_first, near_other, across)):
        for cc in range(2):
            arrived_if(inside(1 - 2 * (d // 2)), near_piece(d, cc), rn.at[1 + 2 * k + cc], sn.at[1 + 2 * k + cc])
    for frame in range(2):
        KV[BAND0 + frame * KB:BAND0 + (frame + 1) * KB, :] = chosen((1 - frame) * HI, KB, band[0, tm * 2 + frame])

    def far_ok(frame, level):
        return inside((1 - 2 * ((frame + level) % 2)) * 2 ** level)

    def near_ok(frame):
        return inside(2 * frame - 1)

    for half_at in range(2):
        frame = mine if half_at == 0 else 1 - mine
        for level in (3, 2, 1):
            k = 3 * half_at + level - 1
            arrived_if(far_ok(frame, level), far_slot(frame, level), rf.at[k], sf.at[k])
    arrived(far_slot(0, 4), rf.at[6], sf.at[6])
    arrived(WO.at[pl.ds(W, W)], rd.at[14], sd.at[14])

    def finish(step, d):
        frame = d // 2
        rows = pl.ds(mo(d * CH, CH), CH)
        tiles = [(mo(frame * HI + i * KB, KB), KB, near_ok(frame)) for i in range(2)]
        tiles += [(mo(BAND0 + frame * KB, TB), KB, near_ok(1 - frame))]
        tiles += [(mo(FAR + frame * 3 * TB + (level - 1) * TB, TB), TB, far_ok(frame, level)) for level in (1, 2, 3)]
        tiles += [(FAR4, TB, far_ok(frame, 4))]
        for h in range(HL):
            lanes = slice(h * HD, (h + 1) * HD)
            lanes_v = slice(W + h * HD, W + (h + 1) * HD)
            top = score_tiles(rows, lanes, tiles)
            m_old = MX[rows, lanes]
            m = jnp.maximum(m_old, jnp.max(top, axis=1, keepdims=True))
            scale = jnp.exp2(m_old - m)
            total, acc = weigh_tiles(tiles, lanes_v, m[:, :1], LS[rows, lanes] * scale, ACC[rows, lanes] * scale)
            AF[step, :, lanes] = (acc / jnp.sum(total, axis=1, keepdims=True)).astype(BF16)
        send(AF.at[step, pl.ds(mo((1 - c) * TB, TB), TB)], A2.at[step, :, pl.ds(W, W)],
             sa.at[step], ra.at[step], d_core)
        A2[step, :, :W] = AF[step, pl.ds(mo(c * TB, TB), TB), :]
        arrived(A2.at[step, :, pl.ds(W, W)], ra.at[step], sa.at[step])

    NB = 512

    def product(step, lo, n, cols):
        return jnp.dot(A2[step, lo:lo + n, :], WO[:, cols], preferred_element_type=F32)

    columns = [slice(i * NB, (i + 1) * NB) for i in range(D // NB)]

    finish(0, across)
    for cols in columns:
        P0[:, cols] = product(0, 0, TB, cols).astype(BF16)
    send(P0.at[pl.ds(0, H)], RU, sr.at[0], rr.at[0], d_right)
    send(P0.at[pl.ds(H, H)], RD, sr.at[1], rr.at[1], d_left)

    finish(1, right)
    for cols in columns:
        P1[:, cols] = product(1, 0, TB, cols).astype(BF16)
    send(P1.at[pl.ds(H, H)], RL.at[pl.ds(H, H)], sr.at[2], rr.at[2], d_right)
    finish(2, left)
    for cols in columns:
        P2[:, cols] = product(2, 0, TB, cols).astype(BF16)
    send(P2.at[pl.ds(0, H)], RR.at[pl.ds(0, H)], sr.at[3], rr.at[3], d_left)

    arrived(RU, rr.at[0], sr.at[0])
    P1[0:H, :] = (P1[0:H, :].astype(F32) + RU[...].astype(F32)).astype(BF16)
    send(P1.at[pl.ds(0, H)], RL.at[pl.ds(0, H)], sr.at[4], rr.at[4], d_right)
    arrived(RD, rr.at[1], sr.at[1])
    P2[H:, :] = (P2[H:, :].astype(F32) + RD[...].astype(F32)).astype(BF16)
    send(P2.at[pl.ds(H, H)], RR.at[pl.ds(H, H)], sr.at[5], rr.at[5], d_left)

    finish(3, x)
    for cols in columns:
        P3[:, cols] = product(3, 0, TB, cols)
    arrived(RL.at[pl.ds(H, H)], rr.at[2], sr.at[2])
    arrived(RR.at[pl.ds(0, H)], rr.at[3], sr.at[3])
    arrived(RL.at[pl.ds(0, H)], rr.at[4], sr.at[4])
    arrived(RR.at[pl.ds(H, H)], rr.at[5], sr.at[5])
    out[...] = (P3[...] + RL[...].astype(F32) + RR[...].astype(F32)).astype(BF16)

    for copy in sent:
        copy.wait_send()
    for here, copy in sent_if:
        @pl.when(here)
        def _(copy=copy):
            copy.wait_send()


def shards(tokens, w_qkv, qk_gain, w_out, band_start):
    w3 = jnp.transpose(w_qkv, (1, 0, 2))
    vmem = pl.BlockSpec(memory_space=pltpu.VMEM)
    hbm = pl.BlockSpec(memory_space=pl.ANY)
    dma = pltpu.SemaphoreType.DMA
    return pl.pallas_call(
        kernel,
        out_shape=jax.ShapeDtypeStruct((TB, D), BF16),
        in_specs=[hbm, hbm, vmem, hbm, pl.BlockSpec(memory_space=pltpu.SMEM)],
        out_specs=vmem,
        scratch_shapes=[
            pltpu.VMEM((ROWS, D), BF16),
            pltpu.VMEM((8 * NR, D), BF16),
            pltpu.VMEM((D, 3 * W), BF16),
            pltpu.VMEM((2 * W, D), BF16),
            pltpu.VMEM((ROWS, W), BF16),
            pltpu.VMEM((KV_ROWS, 2 * W), BF16),
            pltpu.VMEM((7, TB, 2 * W), BF16),
            pltpu.VMEM((ROWS, W), F32),
            pltpu.VMEM((ROWS, W), F32),
            pltpu.VMEM((ROWS, W), F32),
            pltpu.VMEM((CH, 5 * KB), F32),
            pltpu.VMEM((4, CH, W), BF16),
            pltpu.VMEM((4, TB, 2 * W), BF16),
            pltpu.VMEM((TB, D), BF16),
            pltpu.VMEM((TB, D), BF16),
            pltpu.VMEM((TB, D), BF16),
            pltpu.VMEM((TB, D), F32),
            pltpu.VMEM((TB // 2, D), BF16),
            pltpu.VMEM((TB // 2, D), BF16),
            pltpu.VMEM((TB, D), BF16),
            pltpu.VMEM((TB, D), BF16),
            dma((5,)), dma((13,)), dma((13,)), dma((15,)), dma((15,)), dma((9,)), dma((9,)),
            dma((7,)), dma((7,)), dma((4,)), dma((4,)), dma((6,)), dma((6,)),
            pltpu.SemaphoreType.REGULAR((4,)),
        ],
        compiler_params=pltpu.CompilerParams(
            collective_id=0, has_side_effects=True, vmem_limit_bytes=60 * 2**20),
        cost_estimate=pl.CostEstimate(flops=14 * 10**9, bytes_accessed=12 * 10**6, transcendentals=7 * 10**6),
        name="band_attention",
    )(tokens, w3, qk_gain, w_out, jnp.transpose(band_start))


def solution(mesh):
    placed = (P(("tm", "row"), None), P(None, None, "row"), P(None, "row"), P("row", None), P())
    return jax.shard_map(
        shards, mesh=mesh, in_specs=placed, out_specs=P(("tm", "row"), None), check_vma=False
    )
```

```python
import functools
import math

import jax
import jax.numpy as jnp
from jax import lax
from jax.experimental import pallas as pl
from jax.experimental.pallas import tpu as pltpu
from jax.sharding import PartitionSpec as P

MESH = pl.DeviceIdType.MESH
D = 3072
HD = 128
HL = 3
W = HL * HD
TB = 128
CH = 2 * TB
ROWS = 4 * CH
N_TM = 32
LO, OWN, HI, FAR, FAR4, BAND0 = 0, 512, 1536, 2048, 2816, 2944
KV_ROWS = 3456
QSCALE = math.log2(math.e) / math.sqrt(HD)
NEG = -1e30
NR = 112
KB = 256
F32 = jnp.float32
BF16 = jnp.bfloat16


def mo(value, by):
    return pl.multiple_of(value, by)


def kernel(
    tok, w3, gain, wout, band, out,
    G, GH, WQ, WO, Q, KV, FS, ACC, MX, LS, OUT, S, AF, A2, P0, P1, P2, P3, RU, RD, RL, RR,
    loc, sx, rx, sd, rd, sn, rn, sf, rf, sa, ra, sr, rr, known,
):
    tm = lax.axis_index("tm")
    row = lax.axis_index("row")
    x = row // 2
    c = row % 2
    right = (x + 1) % 4
    left = (x + 3) % 4
    across = (x + 2) % 4
    d_right = (tm, right * 2 + c)
    d_left = (tm, left * 2 + c)
    d_core = (tm, x * 2 + (1 - c))

    def d_tm(shift):
        return ((tm + shift + N_TM) % N_TM, row)

    loads = [pltpu.make_async_copy(tok, G.at[pl.ds(mo(row * TB, TB), TB)], loc.at[0])]
    for j in range(3):
        loads.append(pltpu.make_async_copy(w3.at[j], WQ.at[:, pl.ds(j * W, W)], loc.at[1 + j]))
    loads.append(pltpu.make_async_copy(wout, WO.at[pl.ds(0, W)], loc.at[4]))
    for load in loads:
        load.start()

    def signal(semaphore, device):
        pl.semaphore_signal(semaphore, inc=1, device_id=device, device_id_type=MESH)

    KV[FAR:, W:] = jnp.zeros((KV_ROWS - FAR, W), BF16)
    for block in range(4):
        for first in (LO, HI):
            KV[first + block * TB + NR:first + (block + 1) * TB, W:] = jnp.zeros((TB - NR, W), BF16)

    def inside(shift):
        return jnp.logical_and(tm + shift >= 0, tm + shift < N_TM)

    def count(*shifts):
        total = 0
        for shift in shifts:
            total = total + inside(shift).astype(jnp.int32)
        return total

    barrier = pltpu.get_barrier_semaphore()
    for device in (d_right, d_left, d_core):
        signal(barrier, device)

    def signal_tm(semaphore, shift):
        @pl.when(inside(shift))
        def _():
            signal(semaphore, d_tm(shift))

    signal_tm(barrier, 1)
    signal_tm(barrier, -1)
    loads[0].wait()
    pl.semaphore_wait(barrier, 3 + count(1, -1))

    def tell(level):
        signal_tm(known.at[level], 2 ** level)
        signal_tm(known.at[level], -(2 ** level))

    def heard(level):
        pl.semaphore_wait(known.at[level], count(2 ** level, -(2 ** level)))

    def remote(src, dst, send, recv, device):
        return pltpu.make_async_remote_copy(
            src_ref=src, dst_ref=dst, send_sem=send, recv_sem=recv,
            device_id=device, device_id_type=MESH)

    sent = []

    def send(src, dst, send_sem, recv_sem, device):
        copy = remote(src, dst, send_sem, recv_sem, device)
        copy.start()
        sent.append(copy)

    sent_if = []

    def send_if(here, src, dst, send_sem, recv_sem, device):
        copy = remote(src, dst, send_sem, recv_sem, device)

        @pl.when(here)
        def _():
            copy.start()

        sent_if.append((here, copy))

    def arrived_if(here, dst, recv_sem, send_sem):
        @pl.when(here)
        def _():
            arrived(dst, recv_sem, send_sem)

    def arrived(dst, recv_sem, send_sem):
        remote(dst, dst, send_sem, recv_sem, d_core).wait_recv()

    H = TB // 2

    def gather(G, n, base):
        cut = (n // 2 + 15) // 16 * 16

        def block(xx, cc):
            return G.at[pl.ds(mo((xx * 2 + cc) * n, n), n)]

        def half(xx, part, cc=c):
            return G.at[pl.ds(mo((xx * 2 + cc) * n + part * cut, 16), (cut, n - cut)[part])]

        def pass_on(k, xx, part, device=None, k_next=None):
            piece = half(xx, part)
            arrived(piece, rx.at[base + k], sx.at[base + k])
            if device is not None:
                send(piece, piece, sx.at[base + k_next], rx.at[base + k_next], device)
            send(piece, piece, sd.at[base + k], rd.at[base + k], d_core)

        def from_core(k, xx, part):
            arrived(half(xx, part, 1 - c), rd.at[base + k], sd.at[base + k])

        def begin():
            send(half(x, 0), half(x, 0), sx.at[base], rx.at[base], d_right)
            send(half(x, 1), half(x, 1), sx.at[base + 2], rx.at[base + 2], d_left)
            send(block(x, c), block(x, c), sd.at[base + 6], rd.at[base + 6], d_core)
            send(half(x, 1), half(x, 1), sx.at[base + 1], rx.at[base + 1], d_right)
            send(half(x, 0), half(x, 0), sx.at[base + 3], rx.at[base + 3], d_left)

        def first():
            arrived(block(x, 1 - c), rd.at[base + 6], sd.at[base + 6])

        def middle():
            pass_on(0, left, 0, d_right, 4)
            pass_on(2, right, 1, d_left, 5)
            pass_on(1, left, 1)
            pass_on(3, right, 0)

        def middle_core():
            for k, xx, part in ((0, left, 0), (1, left, 1), (2, right, 1), (3, right, 0)):
                from_core(k, xx, part)

        def last():
            pass_on(4, across, 0)
            pass_on(5, across, 1)
            from_core(4, across, 0)
            from_core(5, across, 1)

        return begin, first, middle, middle_core, last

    own = G.at[pl.ds(mo(row * TB, TB), TB)]
    begin, first, middle, middle_core, last = gather(G, TB, 0)
    begin_halo, first_halo, middle_halo, middle_core_halo, last_halo = gather(GH, NR, 7)
    begin()
    tell(0)
    own_halo = GH.at[pl.ds(mo(row * NR, NR), NR)]
    own_part = G.at[pl.ds(mo(row * TB, TB), NR)]
    up = 2 * (x // 2) - 1
    send_if(inside(up), own_part, own_halo, sn.at[0], rn.at[0], d_tm(up))

    @pl.when(jnp.logical_not(inside(-up)))
    def _():
        filler = pltpu.make_async_copy(own_part, own_halo, loc.at[0])
        filler.start()
        filler.wait()


    gq = gain[0:1, :] * QSCALE
    gk = gain[1:2, :]

    def normed(v, gains):
        factor = lax.rsqrt(jnp.mean(v * v, axis=1, keepdims=True) + 1e-6)
        return (v * factor * gains).astype(BF16)

    def project(tokens, n, first_row):
        merged = jnp.dot(tokens, WQ[:, W:], preferred_element_type=F32)
        for cc in range(2):
            rows = pl.ds(mo(first_row + cc * TB, TB), n)
            mine = merged[cc * n:(cc + 1) * n]
            for h in range(HL):
                lanes = slice(h * HD, (h + 1) * HD)
                KV[rows, lanes] = normed(mine[:, lanes], gk[:, lanes])
            KV[rows, W:] = mine[:, W:].astype(BF16)

    def halo_row(d):
        frame = d // 2
        return (1 - frame) * HI + (d - 2 * frame) * CH

    def near_piece(d, cc):
        return KV.at[pl.ds(mo(halo_row(d) + cc * TB + NR, 16), TB - NR)]

    def project_own(k, d):
        project(G[pl.ds(mo(d * CH, CH), CH), :], TB, OWN + d * CH)
        for cc in range(2):
            to = 2 * (d // 2) - 1
            send_if(inside(to), KV.at[pl.ds(mo(OWN + d * CH + cc * TB + NR, 16), TB - NR)], near_piece(d, cc),
                    sn.at[1 + 2 * k + cc], rn.at[1 + 2 * k + cc], d_tm(to))

    def project_halo(d):
        project(GH[pl.ds(mo(d * 2 * NR, 2 * NR), 2 * NR), :], NR, halo_row(d))

    def far_slot(frame, level):
        if level == 4:
            return KV.at[pl.ds(FAR4, TB)]
        return KV.at[pl.ds(mo(FAR + frame * 3 * TB + (level - 1) * TB, TB), TB)]

    def chosen(base, n, first):
        at = [KV[pl.ds(mo(base + i * TB, TB), n), :] for i in range(3)]
        return jnp.where(first == 0, at[0], jnp.where(first == 1, at[1], at[2]))

    def stage_far(frame, level, k, moved_by):
        asking = ((tm + moved_by + N_TM) % N_TM) * 2 + frame
        FS[k] = chosen(OWN + frame * 512, TB, band[level, asking])

    def send_far(half_at, level):
        frame = mine if half_at == 0 else 1 - mine
        moved_by = (2 * ((level + frame) % 2) - 1) * 2 ** level
        k = 3 * half_at + level - 1
        stage_far(frame, level, k, moved_by)
        send_if(inside(moved_by), FS.at[k], far_slot(frame, level), sf.at[k], rf.at[k], d_tm(moved_by))

    frame4 = 1 - tm // 16
    mine = x // 2

    for load in loads[2:4]:
        load.wait()
    first()
    project_own(0, x)
    heard(0)
    tell(1)
    middle()
    heard(1)
    tell(2)
    middle_core()
    near_first = x + 1 - 2 * (x % 2)
    near_other = (near_first + 2) % 4
    project_own(1, near_first)
    send_far(0, 2)
    send_far(0, 1)
    project_own(2, near_other)
    arrived_if(inside(-up), own_halo, rn.at[0], sn.at[0])
    begin_halo()
    heard(2)
    tell(3)
    send_far(0, 3)
    last()
    project_own(3, across)
    send_far(1, 3)
    heard(3)
    stage_far(frame4, 4, 6, 16)
    send(FS.at[6], far_slot(0, 4), sf.at[6], rf.at[6], d_tm(16))
    send_far(1, 2)
    send_far(1, 1)
    loads[4].wait()
    send(WO.at[pl.ds(0, W)], WO.at[pl.ds(W, W)], sd.at[14], rd.at[14], d_core)

    loads[1].wait()

    @pl.loop(0, 2)
    def _(i):
        rows = pl.ds(mo(i * 512, 512), 512)
        merged = jnp.dot(G[rows, :], WQ[:, :W], preferred_element_type=F32)
        for h in range(HL):
            lanes = slice(h * HD, (h + 1) * HD)
            Q[rows, lanes] = normed(merged[:, lanes], gq[:, lanes])

    def score_tiles(rows, lanes, tiles, top=None):
        q = Q[rows, lanes]
        at = 0
        for begins, n, valid in tiles:
            s = lax.dot_general(q, KV[pl.ds(begins, n), lanes], (((1,), (1,)), ((), ())), preferred_element_type=F32)
            if valid is not None:
                s = jnp.where(valid, s, NEG)
            S[:, at:at + n] = s
            at += n
            for i in range(0, n, HD):
                top = s[:, i:i + HD] if top is None else jnp.maximum(top, s[:, i:i + HD])
        return top

    def weigh_tiles(tiles, lanes_v, m, total=None, acc=None):
        at = 0
        for begins, n, _ in tiles:
            p = jnp.exp2(S[:, at:at + n] - m)
            at += n
            for i in range(0, n, HD):
                total = p[:, i:i + HD] if total is None else total + p[:, i:i + HD]
            part = jnp.dot(p.astype(BF16), KV[pl.ds(begins, n), lanes_v], preferred_element_type=F32)
            acc = part if acc is None else acc + part
        return total, acc

    def attend_own(d):
        rows = pl.ds(mo(d * CH, CH), CH)
        tiles = [(OWN + i * KB, KB, None) for i in range(4)]
        for h in range(HL):
            lanes = slice(h * HD, (h + 1) * HD)
            top = score_tiles(rows, lanes, tiles)
            m = jnp.broadcast_to(jnp.max(top, axis=1, keepdims=True), (CH, HD))
            total, acc = weigh_tiles(tiles, slice(W + h * HD, W + (h + 1) * HD), m[:, :1])
            MX[rows, lanes] = m
            LS[rows, lanes] = total
            ACC[rows, lanes] = acc

    pl.loop(0, 2)(attend_own)
    middle_halo()
    pl.loop(2, 4)(attend_own)

    first_halo()
    project_halo(x)
    middle_core_halo()
    project_halo(near_first)
    project_halo(near_other)
    last_halo()
    project_halo(across)
    for k, d in enumerate((x, near_first, near_other, across)):
        for cc in range(2):
            arrived_if(inside(1 - 2 * (d // 2)), near_piece(d, cc), rn.at[1 + 2 * k + cc], sn.at[1 + 2 * k + cc])
    for frame in range(2):
        KV[BAND0 + frame * KB:BAND0 + (frame + 1) * KB, :] = chosen((1 - frame) * HI, KB, band[0, tm * 2 + frame])

    def far_ok(frame, level):
        return inside((1 - 2 * ((frame + level) % 2)) * 2 ** level)

    def near_ok(frame):
        return inside(2 * frame - 1)

    def far_arrived():
        for half_at in range(2):
            frame = mine if half_at == 0 else 1 - mine
            for level in (3, 2, 1):
                k = 3 * half_at + level - 1
                arrived_if(far_ok(frame, level), far_slot(frame, level), rf.at[k], sf.at[k])
        arrived(far_slot(0, 4), rf.at[6], sf.at[6])

    arrived(WO.at[pl.ds(W, W)], rd.at[14], sd.at[14])

    def finish(step, d):
        frame = d // 2
        rows = pl.ds(mo(d * CH, CH), CH)
        near = [(mo(frame * HI + i * KB, KB), KB, near_ok(frame)) for i in range(2)]
        near += [(mo(BAND0 + frame * KB, TB), KB, near_ok(1 - frame))]
        far = [(mo(FAR + frame * 3 * TB + (level - 1) * TB, TB), TB, far_ok(frame, level)) for level in (1, 2, 3)]
        far += [(FAR4, TB, far_ok(frame, 4))]

        def merge(h, tiles):
            lanes = slice(h * HD, (h + 1) * HD)
            top = score_tiles(rows, lanes, tiles)
            m_old = MX[rows, lanes]
            m = jnp.maximum(m_old, jnp.max(top, axis=1, keepdims=True))
            scale = jnp.exp2(m_old - m)
            total, acc = weigh_tiles(tiles, slice(W + h * HD, W + (h + 1) * HD), m[:, :1],
                                     LS[rows, lanes] * scale, ACC[rows, lanes] * scale)
            return lanes, m, total, acc

        if step == 0:
            for h in range(HL):
                lanes, m, total, acc = merge(h, near)
                MX[rows, lanes] = m
                LS[rows, lanes] = total
                ACC[rows, lanes] = acc
            far_arrived()
            near = []
        for h in range(HL):
            lanes, _, total, acc = merge(h, near + far)
            AF[step, :, lanes] = (acc / jnp.sum(total, axis=1, keepdims=True)).astype(BF16)
        send(AF.at[step, pl.ds(mo((1 - c) * TB, TB), TB)], A2.at[step, :, pl.ds(W, W)],
             sa.at[step], ra.at[step], d_core)
        A2[step, :, :W] = AF[step, pl.ds(mo(c * TB, TB), TB), :]

    def exchanged(step):
        arrived(A2.at[step, :, pl.ds(W, W)], ra.at[step], sa.at[step])

    NB = 512

    def product(step, cols, heads=slice(0, 2 * W)):
        return jnp.dot(A2[step, :, heads], WO[heads, cols], preferred_element_type=F32)

    columns = [slice(i * NB, (i + 1) * NB) for i in range(D // NB)]

    finish(0, across)
    for cols in columns:
        P3[:, cols] = product(0, cols, slice(0, W))
    exchanged(0)
    for cols in columns:
        P0[:, cols] = (P3[:, cols] + product(0, cols, slice(W, 2 * W))).astype(BF16)
    send(P0.at[pl.ds(0, H)], RU, sr.at[0], rr.at[0], d_right)
    send(P0.at[pl.ds(H, H)], RD, sr.at[1], rr.at[1], d_left)

    finish(1, right)
    finish(2, left)
    exchanged(1)
    for cols in columns:
        P1[:, cols] = product(1, cols).astype(BF16)
    send(P1.at[pl.ds(H, H)], RL.at[pl.ds(H, H)], sr.at[2], rr.at[2], d_right)
    exchanged(2)
    for cols in columns:
        P2[:, cols] = product(2, cols).astype(BF16)
    send(P2.at[pl.ds(0, H)], RR.at[pl.ds(0, H)], sr.at[3], rr.at[3], d_left)

    arrived(RU, rr.at[0], sr.at[0])
    P1[0:H, :] = (P1[0:H, :].astype(F32) + RU[...].astype(F32)).astype(BF16)
    send(P1.at[pl.ds(0, H)], RL.at[pl.ds(0, H)], sr.at[4], rr.at[4], d_right)
    arrived(RD, rr.at[1], sr.at[1])
    P2[H:, :] = (P2[H:, :].astype(F32) + RD[...].astype(F32)).astype(BF16)
    send(P2.at[pl.ds(H, H)], RR.at[pl.ds(H, H)], sr.at[5], rr.at[5], d_left)

    finish(3, x)
    exchanged(3)
    for cols in columns:
        P3[:, cols] = product(3, cols)
    upper, lower = pl.ds(0, H), pl.ds(H, H)
    arrived(RL.at[lower], rr.at[2], sr.at[2])
    P3[lower, :] += RL[lower, :].astype(F32)
    arrived(RR.at[upper], rr.at[3], sr.at[3])
    P3[upper, :] += RR[upper, :].astype(F32)
    results = []
    for i, (rows, late, sem) in enumerate(((upper, RL, 4), (lower, RR, 5))):
        arrived(late.at[rows], rr.at[sem], sr.at[sem])
        OUT[rows, :] = (P3[rows, :] + late[rows, :].astype(F32)).astype(BF16)
        result = pltpu.make_async_copy(OUT.at[rows], out.at[rows], loc.at[i])
        result.start()
        results.append(result)
    for result in results:
        result.wait()

    for copy in sent:
        copy.wait_send()
    for here, copy in sent_if:
        @pl.when(here)
        def _(copy=copy):
            copy.wait_send()


def shards(tokens, w_qkv, qk_gain, w_out, band_start):
    w3 = jnp.transpose(w_qkv, (1, 0, 2))
    vmem = pl.BlockSpec(memory_space=pltpu.VMEM)
    hbm = pl.BlockSpec(memory_space=pl.ANY)
    dma = pltpu.SemaphoreType.DMA
    return pl.pallas_call(
        kernel,
        out_shape=jax.ShapeDtypeStruct((TB, D), BF16),
        in_specs=[hbm, hbm, vmem, hbm, pl.BlockSpec(memory_space=pltpu.SMEM)],
        out_specs=hbm,
        scratch_shapes=[
            pltpu.VMEM((ROWS, D), BF16),
            pltpu.VMEM((8 * NR, D), BF16),
            pltpu.VMEM((D, 3 * W), BF16),
            pltpu.VMEM((2 * W, D), BF16),
            pltpu.VMEM((ROWS, W), BF16),
            pltpu.VMEM((KV_ROWS, 2 * W), BF16),
            pltpu.VMEM((7, TB, 2 * W), BF16),
            pltpu.VMEM((ROWS, W), F32),
            pltpu.VMEM((ROWS, W), F32),
            pltpu.VMEM((ROWS, W), F32),
            pltpu.VMEM((TB, D), BF16),
            pltpu.VMEM((CH, 5 * KB), F32),
            pltpu.VMEM((4, CH, W), BF16),
            pltpu.VMEM((4, TB, 2 * W), BF16),
            pltpu.VMEM((TB, D), BF16),
            pltpu.VMEM((TB, D), BF16),
            pltpu.VMEM((TB, D), BF16),
            pltpu.VMEM((TB, D), F32),
            pltpu.VMEM((TB // 2, D), BF16),
            pltpu.VMEM((TB // 2, D), BF16),
            pltpu.VMEM((TB, D), BF16),
            pltpu.VMEM((TB, D), BF16),
            dma((5,)), dma((13,)), dma((13,)), dma((15,)), dma((15,)), dma((9,)), dma((9,)),
            dma((7,)), dma((7,)), dma((4,)), dma((4,)), dma((6,)), dma((6,)),
            pltpu.SemaphoreType.REGULAR((4,)),
        ],
        compiler_params=pltpu.CompilerParams(
            collective_id=0, has_side_effects=True, vmem_limit_bytes=60 * 2**20),
        cost_estimate=pl.CostEstimate(flops=14 * 10**9, bytes_accessed=12 * 10**6, transcendentals=7 * 10**6),
        name="band_attention",
    )(tokens, w3, qk_gain, w_out, jnp.transpose(band_start))


def solution(mesh):
    placed = (P(("tm", "row"), None), P(None, None, "row"), P(None, "row"), P("row", None), P())
    return jax.shard_map(
        shards, mesh=mesh, in_specs=placed, out_specs=P(("tm", "row"), None), check_vma=False
    )
```
